32 devices in a mesh: expert: 4 (over y, x), dp: 8 (over z, core).
Axes of the slice: x: 2, y: 2, z: 4, core: 2. Of those that a mesh axis runs over, the one named last changes fastest.
Arguments:
- hidden_rows: bfloat16 [4, 3072, 8192], P('expert', 'dp'), may hold values from -8 to 8
- out_grads: bfloat16 [4, 3072, 2048], P('expert', 'dp'), may hold values from -0.15625 to 0.15625
- counts: int32 [4, 8], P('expert', 'dp'), may hold values from 1 to 384, as said below
- expert_m: bfloat16 [4, 8192, 2048], P('expert', 'dp'), may hold values from -1.75 to 1.75
- expert_v: bfloat16 [4, 8192, 2048], P('expert', 'dp'), may hold values from 0.0029907227 to 0.029907227
- low_rank: bfloat16 [8192, 256], P(('expert', 'dp')), may hold values from -6 to 6
- dt_grads: bfloat16 [8192, 8192], P(('expert', 'dp')), may hold values from -0.0625 to 0.0625
- mamba_m: float32 [8192, 256], P(('expert', 'dp')), may hold values from -1.75 to 1.75
- mamba_v: float32 [8192, 256], P(('expert', 'dp')), may hold values from 0.003 to 0.03
Outputs:
- expert_m_new: bfloat16 [4, 8192, 2048], P('expert', 'dp')
- expert_v_new: bfloat16 [4, 8192, 2048], P('expert', 'dp')
- expert_step: bfloat16 [4, 8192, 2048], P('expert', 'dp')
- mamba_m_new: float32 [8192, 256], P(('expert', 'dp'))
- mamba_v_new: float32 [8192, 256], P(('expert', 'dp'))
- mamba_step: float32 [8192, 256], P(('expert', 'dp'))
The draws below stay inside these ranges and needn't reach their ends.
Inputs may be any that keep to these rules, and one draw needn't show every extreme that they name: counts[e, d] is the number of live rows at the front of the 384 slots of block d of expert e; some block of every draw is full.
All inputs are finite; a program needn't handle non-finite values.
Results may differ from the reference program's by a relative error of at most 0.006.
Values may be sent and summed in bfloat16 or wider, within the bound.
A program may use at most 192 MiB of HBM per device.

```python
import math
import jax
import jax.numpy as jnp
from jax import lax

FF_WIN = 8192
D_WIN = 2048
INNER = 8192
DT_RANK = 256
STEP = 20
CAP = 384
EXPERTS = 4
TOKENS_M = 8192
N_DP = 8


def draw_counts(key, part):
    key = jax.random.fold_in(key, 7)
    key_base, key_full, key_pick = jax.random.split(key, 3)
    base = jax.random.randint(key_base, (EXPERTS, N_DP), 1, CAP // 3 + 1)
    full = jax.random.randint(key_full, (EXPERTS, N_DP), 0, 8) == 0
    chosen = jax.random.randint(key_pick, (), 0, EXPERTS * N_DP)
    places = jnp.arange(EXPERTS * N_DP, dtype=jnp.int32).reshape(EXPERTS, N_DP)
    return jnp.where(full | (places == chosen), CAP, base).astype(jnp.int32)


def spiked(result, own_key, source, target, blocks, factor):
    owner, partner = [(jnp.arange(result.shape[position]) // (result.shape[position] // blocks)).reshape([-1 if axis == position else 1 for axis in range(result.ndim)]) for position in (source, target)]
    chosen = jax.random.permutation(own_key, blocks)[partner]
    strong = (owner == chosen) | (owner == (partner + blocks // 2) % blocks)
    return jnp.where(strong, factor * result, result)


def shard_levels(own_key, dims, pieces, low, largest):
    def one(dim, blocks):
        draws = jax.random.uniform(jax.random.fold_in(jax.random.fold_in(own_key, 6), dim), (blocks,), jnp.float32, low / len(pieces), largest / len(pieces))
        return jnp.repeat(jnp.exp(draws), dims[dim] // blocks).reshape((-1,) + (1,) * (len(dims) - dim - 1))

    level = one(*pieces[0])
    for cut in pieces[1:]:
        level = level * one(*cut)
    return level


def centred(own_key, shape, scale, reach, pieces=(), kind=jnp.bfloat16):
    values = jax.random.normal(own_key, shape, jnp.float32) * scale
    if len(pieces) > 0:
        values = shard_levels(own_key, shape, pieces, -0.22, 0.18) * values
    return jnp.clip(values, min=-reach, max=reach).astype(kind)


def noise_with(own_key, extent, width, bound, cuts, heavy, kind=jnp.bfloat16):
    result = width * jax.random.normal(own_key, extent, jnp.float32)
    if cuts:
        result = result * shard_levels(own_key, extent, cuts, -0.22, 0.18)
    return jnp.clip(spiked(result, jax.random.fold_in(own_key, 3), *heavy), -bound, bound).astype(kind)


def setup_inputs(seed: int = 0) -> dict:
    seeds = jax.random.split(jax.random.key(seed), 10)
    return {
        "hidden_rows": noise_with(seeds[0], (EXPERTS, N_DP * CAP, FF_WIN), 1.0, 8.0, ((0, 4), (1, 8)), (1, 2, 8, 2.0)),
        "out_grads": centred(seeds[1], (EXPERTS, N_DP * CAP, D_WIN), 0.025, 0.15625, ((0, 4), (1, 8))),
        "counts": draw_counts(jax.random.fold_in(seeds[9], 71), 0),
        "expert_m": centred(seeds[3], (EXPERTS, FF_WIN, D_WIN), 0.3, 1.75, ((0, 4), (1, 8))),
        "expert_v": jnp.clip(jnp.exp(math.log(0.029907227) - 2.3025851 * jax.random.uniform(seeds[4], (EXPERTS, FF_WIN, D_WIN), jnp.float32) ** shard_levels(seeds[4], (EXPERTS, FF_WIN, D_WIN), ((0, 4), (1, 8)), -0.2, 0.2)), 0.0029907227, 0.029907227).astype(jnp.bfloat16),
        "low_rank": centred(seeds[5], (TOKENS_M, DT_RANK), 1.0, 6.0, ((0, 32),)),
        "dt_grads": noise_with(seeds[6], (TOKENS_M, INNER), 0.0055, 0.0625, ((0, 32),), (0, 1, 32, 2.75)),
        "mamba_m": centred(seeds[7], (INNER, DT_RANK), 0.3, 1.75, ((0, 32),), jnp.float32),
        "mamba_v": jnp.clip(jnp.exp(math.log(0.03) - 2.3025851 * jax.random.uniform(seeds[8], (INNER, DT_RANK), jnp.float32) ** shard_levels(seeds[8], (INNER, DT_RANK), ((0, 32),), -0.2, 0.2)), 0.003, 0.03),
    }


def adam_update(moment_old, second_old, gradient):
    moment_one = 0.9 * moment_old.astype(jnp.float32) + 0.1 * gradient
    second = 0.999 * second_old.astype(jnp.float32) + 0.001 * gradient * gradient
    direction = moment_one / (1.0 - 0.9 ** STEP) / (jnp.sqrt(second / (1.0 - 0.999 ** STEP)) + 1e-08)
    return (moment_one, second, direction)

def expert_sum(hidden_block, out_block, live_counts):
    hidden_parts = hidden_block.reshape(N_DP, CAP, FF_WIN)
    out_parts = out_block.reshape(N_DP, CAP, D_WIN)
    positions = jnp.arange(CAP, dtype=jnp.int32)[:, None]

    def accumulate(summed, parts):
        hidden_part, out_part, live_rows = parts
        masked = jnp.where(positions < live_rows, out_part, jnp.zeros_like(out_part))
        product = jnp.dot(hidden_part.T, masked, preferred_element_type=jnp.float32)
        rounded = lax.optimization_barrier(product.astype(jnp.bfloat16))
        return (summed + rounded.astype(jnp.float32), None)
    summed, unused = lax.scan(accumulate, jnp.zeros((FF_WIN, D_WIN), jnp.float32), (hidden_parts, out_parts, live_counts))
    return summed

def reference(hidden_rows, out_grads, counts, expert_m, expert_v, low_rank, dt_grads, mamba_m, mamba_v):
    expert_grad = lax.map(lambda parts: expert_sum(parts[0], parts[1], parts[2]), (hidden_rows, out_grads, counts))
    moment_one, second, direction = adam_update(expert_m, expert_v, expert_grad)
    mamba_grad = jnp.dot(dt_grads.T, low_rank, preferred_element_type=jnp.float32)
    mamba_one, mamba_two, mamba_dir = adam_update(mamba_m, mamba_v, mamba_grad)
    return (moment_one.astype(jnp.bfloat16), second.astype(jnp.bfloat16), direction.astype(jnp.bfloat16), mamba_one, mamba_two, mamba_dir)
```

```python
import functools

import jax
import jax.numpy as jnp
from jax import lax
from jax.experimental import pallas as pl
from jax.experimental.pallas import tpu as pltpu
from jax.sharding import PartitionSpec as P

STEP = 20
MESH = pl.DeviceIdType.MESH


def adam_update(moment_old, second_old, gradient):
    moment_one = 0.9 * moment_old.astype(jnp.float32) + 0.1 * gradient
    second = 0.999 * second_old.astype(jnp.float32) + 0.001 * gradient * gradient
    direction = moment_one / (1.0 - 0.9**STEP) / (jnp.sqrt(second / (1.0 - 0.999**STEP)) + 1e-08)
    return (moment_one, second, direction)


def expert_kernel(
    n, count_ref, h_ref, o_ref, acc, hid, outs, hid_send, hid_recv, line_send, sib_send, out_recv, own_sem
):
    chips = n // 2
    d = lax.axis_index("dp")
    p, c = d // 2, d % 2
    sibling = 2 * p + 1 - c
    capacity = o_ref.shape[0]
    cols = hid.shape[2]

    def columns(t):
        return pl.ds(pl.multiple_of(t * cols, cols), cols)

    own = pltpu.make_async_copy(h_ref.at[:, columns(d)], hid.at[d], own_sem)
    own.start()
    positions = lax.broadcasted_iota(jnp.int32, o_ref.shape, 0)
    value = o_ref[...]
    outs[d] = jnp.where(positions < count_ref[0, 0], value, jnp.zeros_like(value))

    barrier = pltpu.get_barrier_semaphore()
    for k in range(1, n):
        pl.semaphore_signal(barrier, inc=1, device_id={"dp": (d + k) % n}, device_id_type=MESH)
    pl.semaphore_wait(barrier, n - 1)

    def line_copy(side, q):
        s = 2 * q + c
        return pltpu.make_async_remote_copy(
            src_ref=outs.at[s],
            dst_ref=outs.at[s],
            send_sem=line_send.at[side, q],
            recv_sem=out_recv.at[s],
            device_id={"dp": d + (2 if side else -2)},
            device_id_type=MESH,
        )

    def sib_copy(q):
        s = 2 * q + c
        return pltpu.make_async_remote_copy(
            src_ref=outs.at[s],
            dst_ref=outs.at[s],
            send_sem=sib_send.at[q],
            recv_sem=out_recv.at[s],
            device_id={"dp": sibling},
            device_id_type=MESH,
        )

    def out_arrival(s):
        return pltpu.make_async_copy(outs.at[s], outs.at[s], out_recv.at[s])

    def hid_copy(t):
        return pltpu.make_async_remote_copy(
            src_ref=h_ref.at[:, columns(t)],
            dst_ref=hid.at[d],
            send_sem=hid_send.at[t],
            recv_sem=hid_recv.at[d],
            device_id={"dp": t},
            device_id_type=MESH,
        )

    def hid_arrival(s):
        return pltpu.make_async_copy(hid.at[s], hid.at[s], hid_recv.at[s])

    @pl.when(p < chips - 1)
    def _():
        line_copy(1, p).start()

    @pl.when(p > 0)
    def _():
        line_copy(0, p).start()

    sib_copy(p).start()
    hid_copy(sibling).start()
    for k in range(1, chips):
        for sign in (-1, 1):
            q = p + sign * k

            @pl.when(jnp.logical_and(q >= 0, q < chips))
            def _(q=q):
                hid_copy(2 * q + c).start()
                hid_copy(2 * q + 1 - c).start()

    acc[...] = jnp.zeros_like(acc)

    rows = min(256, cols)
    width = 512

    def multiply(s):
        @pl.loop(0, cols // rows)
        def _(i):
            at = pl.ds(pl.multiple_of(i * rows, rows), rows)
            left = hid[s, :, at]

            for j in range(acc.shape[1] // width):
                wide = pl.ds(j * width, width)
                acc[at, wide] += lax.dot_general(
                    left,
                    outs[s, :, wide],
                    (((0,), (0,)), ((), ())),
                    preferred_element_type=jnp.float32,
                )

    def forward(k):
        left, right = p - k, p + k

        @pl.when(left >= 0)
        def _():
            out_arrival(2 * left + c).wait()

            @pl.when(p < chips - 1)
            def _():
                line_copy(1, left).start()

            sib_copy(left).start()

        @pl.when(right < chips)
        def _():
            out_arrival(2 * right + c).wait()

            @pl.when(p > 0)
            def _():
                line_copy(0, right).start()

            sib_copy(right).start()

    def multiply_at(k):
        @pl.loop(0, 4)
        def _(j):
            q = p + (2 * (j // 2) - 1) * k
            cc = (c + j) % 2

            @pl.when(jnp.logical_and(q >= 0, q < chips))
            def _():
                s = 2 * q + cc

                @pl.when(cc != c)
                def _():
                    out_arrival(s).wait()

                hid_arrival(s).wait()
                multiply(s)

    own.wait()
    multiply(d)
    out_arrival(sibling).wait()
    hid_arrival(sibling).wait()
    multiply(sibling)

    @pl.loop(1, chips + 1)
    def _(k):
        @pl.when(k < chips)
        def _():
            forward(k)

        @pl.when(k > 1)
        def _():
            multiply_at(k - 1)

    @pl.loop(0, chips)
    def _(q):
        sib_copy(q).wait_send()

        @pl.when(jnp.logical_and(q <= p, p < chips - 1))
        def _():
            line_copy(1, q).wait_send()

        @pl.when(jnp.logical_and(q >= p, p > 0))
        def _():
            line_copy(0, q).wait_send()

    @pl.loop(1, n)
    def _(k):
        hid_copy((d + k) % n).wait_send()


def expert_gradient(n, counts, hidden, out_rows):
    capacity, total = hidden.shape
    width = out_rows.shape[1]
    cols = total // n
    chips = n // 2
    return pl.pallas_call(
        functools.partial(expert_kernel, n),
        out_shape=jax.ShapeDtypeStruct((cols, width), jnp.float32),
        in_specs=[
            pl.BlockSpec(memory_space=pltpu.SMEM),
            pl.BlockSpec(memory_space=pl.ANY),
            pl.BlockSpec(memory_space=pltpu.VMEM),
        ],
        out_specs=pl.BlockSpec(memory_space=pltpu.VMEM),
        scratch_shapes=[
            pltpu.VMEM((n, capacity, cols), jnp.bfloat16),
            pltpu.VMEM((n, capacity, width), jnp.bfloat16),
            pltpu.SemaphoreType.DMA((n,)),
            pltpu.SemaphoreType.DMA((n,)),
            pltpu.SemaphoreType.DMA((2, chips)),
            pltpu.SemaphoreType.DMA((chips,)),
            pltpu.SemaphoreType.DMA((n,)),
            pltpu.SemaphoreType.DMA,
        ],
        compiler_params=pltpu.CompilerParams(
            collective_id=0, has_side_effects=True, vmem_limit_bytes=52 * 2**20
        ),
        cost_estimate=pl.CostEstimate(
            flops=2 * n * capacity * cols * width, bytes_accessed=600 * 2**20, transcendentals=0
        ),
    )(counts, hidden, out_rows)


def body(n, hidden_rows, out_grads, counts, expert_m, expert_v, low_rank, dt_grads, mamba_m, mamba_v):
    contract = (((0,), (0,)), ((), ()))
    mamba_grad = lax.psum_scatter(
        lax.dot_general(dt_grads, low_rank, contract, preferred_element_type=jnp.float32).astype(
            jnp.bfloat16
        ),
        ("expert", "dp"),
        scatter_dimension=0,
        tiled=True,
    ).astype(jnp.float32)
    expert_grad = expert_gradient(n, counts, hidden_rows[0], out_grads[0])
    moment_one, second, direction = adam_update(expert_m[0], expert_v[0], expert_grad)
    mamba_one, mamba_two, mamba_dir = adam_update(mamba_m, mamba_v, mamba_grad)
    return (
        moment_one.astype(jnp.bfloat16)[None],
        second.astype(jnp.bfloat16)[None],
        direction.astype(jnp.bfloat16)[None],
        mamba_one,
        mamba_two,
        mamba_dir,
    )


def solution(mesh):
    in_specs = (
        P("expert", "dp", None),
        P("expert", "dp", None),
        P("expert", "dp"),
        P("expert", "dp", None),
        P("expert", "dp", None),
        P(("expert", "dp"), None),
        P(("expert", "dp"), None),
        P(("expert", "dp"), None),
        P(("expert", "dp"), None),
    )
    out_specs = (
        P("expert", "dp", None),
        P("expert", "dp", None),
        P("expert", "dp", None),
        P(("expert", "dp"), None),
        P(("expert", "dp"), None),
        P(("expert", "dp"), None),
    )
    return jax.shard_map(
        functools.partial(body, mesh.shape["dp"]),
        mesh=mesh,
        in_specs=in_specs,
        out_specs=out_specs,
        check_vma=False,
    )
```

```python
import functools

import jax
import jax.numpy as jnp
from jax import lax
from jax.experimental import pallas as pl
from jax.experimental.pallas import tpu as pltpu
from jax.sharding import PartitionSpec as P

STEP = 20
MESH = pl.DeviceIdType.MESH


def adam_update(moment_old, second_old, gradient):
    moment_one = 0.9 * moment_old.astype(jnp.float32) + 0.1 * gradient
    second = 0.999 * second_old.astype(jnp.float32) + 0.001 * gradient * gradient
    direction = moment_one / (1.0 - 0.9**STEP) / (jnp.sqrt(second / (1.0 - 0.999**STEP)) + 1e-08)
    return (moment_one, second, direction)


def expert_kernel(
    n,
    groups,
    count_ref,
    h_ref,
    o_ref,
    g_ref,
    acc,
    total,
    hid,
    outs,
    first,
    first_sum,
    second,
    second_sum,
    third,
    hid_send,
    hid_recv,
    line_send,
    sib_send,
    out_recv,
    own_sem,
    first_send,
    first_recv,
    second_send,
    second_recv,
    third_send,
    third_recv,
):
    chips = n // 2
    d = lax.axis_index("dp")
    e = lax.axis_index("expert")
    p, c = d // 2, d % 2
    sibling = 2 * p + 1 - c
    capacity = o_ref.shape[0]
    cols = hid.shape[2]

    def columns(t):
        return pl.ds(pl.multiple_of(t * cols, cols), cols)

    own = pltpu.make_async_copy(h_ref.at[:, columns(d)], hid.at[d], own_sem)
    own.start()
    positions = lax.broadcasted_iota(jnp.int32, o_ref.shape, 0)
    value = o_ref[...]
    outs[d] = jnp.where(positions < count_ref[0, 0], value, jnp.zeros_like(value))

    barrier = pltpu.get_barrier_semaphore()
    for k in range(1, n):
        pl.semaphore_signal(barrier, inc=1, device_id={"dp": (d + k) % n}, device_id_type=MESH)
    for k in range(1, groups):
        pl.semaphore_signal(
            barrier, inc=1, device_id={"expert": (e + k) % groups}, device_id_type=MESH
        )
    pl.semaphore_wait(barrier, n + groups - 2)

    def line_copy(side, q):
        s = 2 * q + c
        return pltpu.make_async_remote_copy(
            src_ref=outs.at[s],
            dst_ref=outs.at[s],
            send_sem=line_send.at[side, q],
            recv_sem=out_recv.at[s],
            device_id={"dp": d + (2 if side else -2)},
            device_id_type=MESH,
        )

    def sib_copy(q):
        s = 2 * q + c
        return pltpu.make_async_remote_copy(
            src_ref=outs.at[s],
            dst_ref=outs.at[s],
            send_sem=sib_send.at[q],
            recv_sem=out_recv.at[s],
            device_id={"dp": sibling},
            device_id_type=MESH,
        )

    def out_arrival(s):
        return pltpu.make_async_copy(outs.at[s], outs.at[s], out_recv.at[s])

    def hid_copy(t):
        return pltpu.make_async_remote_copy(
            src_ref=h_ref.at[:, columns(t)],
            dst_ref=hid.at[d],
            send_sem=hid_send.at[t],
            recv_sem=hid_recv.at[d],
            device_id={"dp": t},
            device_id_type=MESH,
        )

    def hid_arrival(s):
        return pltpu.make_async_copy(hid.at[s], hid.at[s], hid_recv.at[s])

    span = g_ref.shape[0] // groups
    block = total.shape[0]

    def first_copy(t):
        return pltpu.make_async_remote_copy(
            src_ref=g_ref.at[pl.ds(pl.multiple_of(t * span, span), span), :],
            dst_ref=first.at[e],
            send_sem=first_send.at[t],
            recv_sem=first_recv.at[e],
            device_id={"expert": t},
            device_id_type=MESH,
        )

    def second_copy():
        return pltpu.make_async_remote_copy(
            src_ref=first_sum.at[:, 1 - c],
            dst_ref=second,
            send_sem=second_send,
            recv_sem=second_recv,
            device_id={"dp": sibling},
            device_id_type=MESH,
        )

    def third_copy(q):
        return pltpu.make_async_remote_copy(
            src_ref=second_sum.at[q],
            dst_ref=third.at[p],
            send_sem=third_send.at[q],
            recv_sem=third_recv.at[p],
            device_id={"dp": 2 * q + c},
            device_id_type=MESH,
        )

    def arrival(buffer, sem, at):
        return pltpu.make_async_copy(buffer.at[at], buffer.at[at], sem.at[at])

    def finish_first():
        for k in range(1, groups):
            arrival(first, first_recv, (e + k) % groups).wait()

        @pl.loop(0, n)
        def _(t):
            summed = g_ref[
                pl.ds(pl.multiple_of(e * span + t * block, block), block), :
            ].astype(jnp.float32)
            for k in range(1, groups):
                summed += first[
                    (e + k) % groups, pl.ds(pl.multiple_of(t * block, block), block), :
                ].astype(jnp.float32)
            first_sum[t // 2, t % 2] = summed.astype(jnp.bfloat16)

        second_copy().start()

    def finish_second():
        pltpu.make_async_copy(second, second, second_recv).wait()

        @pl.loop(0, chips)
        def _(q):
            second_sum[q] = (
                first_sum[q, c].astype(jnp.float32) + second[q].astype(jnp.float32)
            ).astype(jnp.bfloat16)

        for k in range(1, chips):
            third_copy((p + k) % chips).start()

    def finish_third():
        summed = second_sum[p].astype(jnp.float32)
        for k in range(1, chips):
            q = (p + k) % chips
            arrival(third, third_recv, q).wait()
            summed += third[q].astype(jnp.float32)
        total[...] = summed

    @pl.when(p < chips - 1)
    def _():
        line_copy(1, p).start()

    @pl.when(p > 0)
    def _():
        line_copy(0, p).start()

    for k in range(1, groups):
        first_copy((e + k) % groups).start()
    sib_copy(p).start()
    hid_copy(sibling).start()

    def hid_start(k):
        for sign in (-1, 1):
            q = p + sign * k

            @pl.when(jnp.logical_and(q >= 0, q < chips))
            def _(q=q):
                hid_copy(2 * q + c).start()
                hid_copy(2 * q + 1 - c).start()

    hid_start(1)

    acc[...] = jnp.zeros_like(acc)

    rows = min(256, cols)
    width = 512

    def multiply(s):
        @pl.loop(0, cols // rows)
        def _(i):
            at = pl.ds(pl.multiple_of(i * rows, rows), rows)
            left = hid[s, :, at]

            for j in range(acc.shape[1] // width):
                wide = pl.ds(j * width, width)
                acc[at, wide] += lax.dot_general(
                    left,
                    outs[s, :, wide],
                    (((0,), (0,)), ((), ())),
                    preferred_element_type=jnp.float32,
                )

    def forward(k):
        left, right = p - k, p + k

        @pl.when(left >= 0)
        def _():
            out_arrival(2 * left + c).wait()

            @pl.when(p < chips - 1)
            def _():
                line_copy(1, left).start()

            sib_copy(left).start()

        @pl.when(right < chips)
        def _():
            out_arrival(2 * right + c).wait()

            @pl.when(p > 0)
            def _():
                line_copy(0, right).start()

            sib_copy(right).start()

    def multiply_at(k):
        @pl.loop(0, 4)
        def _(j):
            q = p + (2 * (j // 2) - 1) * k
            cc = (c + j) % 2

            @pl.when(jnp.logical_and(q >= 0, q < chips))
            def _():
                s = 2 * q + cc

                @pl.when(cc != c)
                def _():
                    out_arrival(s).wait()

                hid_arrival(s).wait()
                multiply(s)

    own.wait()
    multiply(d)
    out_arrival(sibling).wait()
    hid_arrival(sibling).wait()
    multiply(sibling)

    @pl.loop(1, chips + 1)
    def _(k):
        @pl.when(k < chips)
        def _():
            forward(k)

            @pl.when(k < chips - 1)
            def _():
                hid_start(k + 1)

        @pl.when(k == 1)
        def _():
            finish_first()

        @pl.when(k == 2)
        def _():
            finish_second()

        @pl.when(k > 1)
        def _():
            multiply_at(k - 1)

    finish_third()

    @pl.loop(0, chips)
    def _(q):
        sib_copy(q).wait_send()

        @pl.when(jnp.logical_and(q <= p, p < chips - 1))
        def _():
            line_copy(1, q).wait_send()

        @pl.when(jnp.logical_and(q >= p, p > 0))
        def _():
            line_copy(0, q).wait_send()

    @pl.loop(1, n)
    def _(k):
        hid_copy((d + k) % n).wait_send()

    for k in range(1, groups):
        first_copy((e + k) % groups).wait_send()
    second_copy().wait_send()
    for k in range(1, chips):
        third_copy((p + k) % chips).wait_send()


def gradients(n, groups, counts, hidden, out_rows, mamba_part):
    capacity, total = hidden.shape
    width = out_rows.shape[1]
    cols = total // n
    chips = n // 2
    inner, rank = mamba_part.shape
    block = inner // (n * groups)
    return pl.pallas_call(
        functools.partial(expert_kernel, n, groups),
        out_shape=(
            jax.ShapeDtypeStruct((cols, width), jnp.float32),
            jax.ShapeDtypeStruct((block, rank), jnp.float32),
        ),
        in_specs=[
            pl.BlockSpec(memory_space=pltpu.SMEM),
            pl.BlockSpec(memory_space=pl.ANY),
            pl.BlockSpec(memory_space=pltpu.VMEM),
            pl.BlockSpec(memory_space=pltpu.VMEM),
        ],
        out_specs=(
            pl.BlockSpec(memory_space=pltpu.VMEM),
            pl.BlockSpec(memory_space=pltpu.VMEM),
        ),
        scratch_shapes=[
            pltpu.VMEM((n, capacity, cols), jnp.bfloat16),
            pltpu.VMEM((n, capacity, width), jnp.bfloat16),
            pltpu.VMEM((groups, inner // groups, rank), jnp.bfloat16),
            pltpu.VMEM((chips, 2, block, rank), jnp.bfloat16),
            pltpu.VMEM((chips, block, rank), jnp.bfloat16),
            pltpu.VMEM((chips, block, rank), jnp.bfloat16),
            pltpu.VMEM((chips, block, rank), jnp.bfloat16),
            pltpu.SemaphoreType.DMA((n,)),
            pltpu.SemaphoreType.DMA((n,)),
            pltpu.SemaphoreType.DMA((2, chips)),
            pltpu.SemaphoreType.DMA((chips,)),
            pltpu.SemaphoreType.DMA((n,)),
            pltpu.SemaphoreType.DMA,
            pltpu.SemaphoreType.DMA((groups,)),
            pltpu.SemaphoreType.DMA((groups,)),
            pltpu.SemaphoreType.DMA,
            pltpu.SemaphoreType.DMA,
            pltpu.SemaphoreType.DMA((chips,)),
            pltpu.SemaphoreType.DMA((chips,)),
        ],
        compiler_params=pltpu.CompilerParams(
            collective_id=0, has_side_effects=True, vmem_limit_bytes=52 * 2**20
        ),
        cost_estimate=pl.CostEstimate(
            flops=2 * n * capacity * cols * width, bytes_accessed=600 * 2**20, transcendentals=0
        ),
    )(counts, hidden, out_rows, mamba_part)


def body(
    n, groups, hidden_rows, out_grads, counts, expert_m, expert_v, low_rank, dt_grads, mamba_m, mamba_v
):
    contract = (((0,), (0,)), ((), ()))
    mamba_part = lax.dot_general(
        dt_grads, low_rank, contract, preferred_element_type=jnp.float32
    ).astype(jnp.bfloat16)
    expert_grad, mamba_grad = gradients(
        n, groups, counts, hidden_rows[0], out_grads[0], mamba_part
    )
    moment_one, second, direction = adam_update(expert_m[0], expert_v[0], expert_grad)
    mamba_one, mamba_two, mamba_dir = adam_update(mamba_m, mamba_v, mamba_grad)
    return (
        moment_one.astype(jnp.bfloat16)[None],
        second.astype(jnp.bfloat16)[None],
        direction.astype(jnp.bfloat16)[None],
        mamba_one,
        mamba_two,
        mamba_dir,
    )


def solution(mesh):
    in_specs = (
        P("expert", "dp", None),
        P("expert", "dp", None),
        P("expert", "dp"),
        P("expert", "dp", None),
        P("expert", "dp", None),
        P(("expert", "dp"), None),
        P(("expert", "dp"), None),
        P(("expert", "dp"), None),
        P(("expert", "dp"), None),
    )
    out_specs = (
        P("expert", "dp", None),
        P("expert", "dp", None),
        P("expert", "dp", None),
        P(("expert", "dp"), None),
        P(("expert", "dp"), None),
        P(("expert", "dp"), None),
    )
    return jax.shard_map(
        functools.partial(body, mesh.shape["dp"], mesh.shape["expert"]),
        mesh=mesh,
        in_specs=in_specs,
        out_specs=out_specs,
        check_vma=False,
    )
```

```python
import functools

import jax
import jax.numpy as jnp
from jax import lax
from jax.experimental import pallas as pl
from jax.experimental.pallas import tpu as pltpu
from jax.sharding import PartitionSpec as P

STEP = 20
MESH = pl.DeviceIdType.MESH


def adam_update(moment_old, second_old, gradient):
    moment_one = 0.9 * moment_old.astype(jnp.float32) + 0.1 * gradient
    second = 0.999 * second_old.astype(jnp.float32) + 0.001 * gradient * gradient
    direction = moment_one / (1.0 - 0.9**STEP) / (jnp.sqrt(second / (1.0 - 0.999**STEP)) + 1e-08)
    return (moment_one, second, direction)


def expert_kernel(
    n,
    groups,
    count_ref,
    h_ref,
    o_ref,
    dt_ref,
    low_ref,
    acc,
    total,
    hid,
    outs,
    first,
    first_sum,
    second,
    second_sum,
    third,
    g_ref,
    hid_send,
    hid_recv,
    line_send,
    sib_send,
    out_recv,
    own_sem,
    first_send,
    first_recv,
    second_send,
    second_recv,
    third_send,
    third_recv,
):
    chips = n // 2
    d = lax.axis_index("dp")
    e = lax.axis_index("expert")
    p, c = d // 2, d % 2
    sibling = 2 * p + 1 - c
    capacity = o_ref.shape[0]
    cols = hid.shape[2]

    def columns(t):
        return pl.ds(pl.multiple_of(t * cols, cols), cols)

    own = pltpu.make_async_copy(h_ref.at[:, columns(d)], hid.at[d], own_sem)
    own.start()
    positions = lax.broadcasted_iota(jnp.int32, o_ref.shape, 0)
    value = o_ref[...]
    outs[d] = jnp.where(positions < count_ref[0, 0], value, jnp.zeros_like(value))

    barrier = pltpu.get_barrier_semaphore()
    for k in range(1, n):
        pl.semaphore_signal(barrier, inc=1, device_id={"dp": (d + k) % n}, device_id_type=MESH)
    for k in range(1, groups):
        pl.semaphore_signal(
            barrier, inc=1, device_id={"expert": (e + k) % groups}, device_id_type=MESH
        )
    pl.semaphore_wait(barrier, n + groups - 2)

    def line_copy(side, q):
        s = 2 * q + c
        return pltpu.make_async_remote_copy(
            src_ref=outs.at[s],
            dst_ref=outs.at[s],
            send_sem=line_send.at[side, q],
            recv_sem=out_recv.at[s],
            device_id={"dp": d + (2 if side else -2)},
            device_id_type=MESH,
        )

    def sib_copy(q):
        s = 2 * q + c
        return pltpu.make_async_remote_copy(
            src_ref=outs.at[s],
            dst_ref=outs.at[s],
            send_sem=sib_send.at[q],
            recv_sem=out_recv.at[s],
            device_id={"dp": sibling},
            device_id_type=MESH,
        )

    def out_arrival(s):
        return pltpu.make_async_copy(outs.at[s], outs.at[s], out_recv.at[s])

    def hid_copy(t):
        return pltpu.make_async_remote_copy(
            src_ref=h_ref.at[:, columns(t)],
            dst_ref=hid.at[d],
            send_sem=hid_send.at[t],
            recv_sem=hid_recv.at[d],
            device_id={"dp": t},
            device_id_type=MESH,
        )

    def hid_arrival(s):
        return pltpu.make_async_copy(hid.at[s], hid.at[s], hid_recv.at[s])

    span = g_ref.shape[0] // groups
    block = total.shape[0]

    def first_copy(t):
        return pltpu.make_async_remote_copy(
            src_ref=g_ref.at[pl.ds(pl.multiple_of(t * span, span), span), :],
            dst_ref=first.at[e],
            send_sem=first_send.at[t],
            recv_sem=first_recv.at[e],
            device_id={"expert": t},
            device_id_type=MESH,
        )

    def second_copy():
        return pltpu.make_async_remote_copy(
            src_ref=first_sum.at[:, 1 - c],
            dst_ref=second,
            send_sem=second_send,
            recv_sem=second_recv,
            device_id={"dp": sibling},
            device_id_type=MESH,
        )

    def third_copy(q):
        return pltpu.make_async_remote_copy(
            src_ref=second_sum.at[q],
            dst_ref=third.at[p],
            send_sem=third_send.at[q],
            recv_sem=third_recv.at[p],
            device_id={"dp": 2 * q + c},
            device_id_type=MESH,
        )

    def arrival(buffer, sem, at):
        return pltpu.make_async_copy(buffer.at[at], buffer.at[at], sem.at[at])

    def finish_first():
        for k in range(1, groups):
            arrival(first, first_recv, (e + k) % groups).wait()

        @pl.loop(0, n)
        def _(t):
            summed = g_ref[
                pl.ds(pl.multiple_of(e * span + t * block, block), block), :
            ].astype(jnp.float32)
            for k in range(1, groups):
                summed += first[
                    (e + k) % groups, pl.ds(pl.multiple_of(t * block, block), block), :
                ].astype(jnp.float32)
            first_sum[t // 2, t % 2] = summed.astype(jnp.bfloat16)

        second_copy().start()

    def finish_second():
        pltpu.make_async_copy(second, second, second_recv).wait()

        @pl.loop(0, chips)
        def _(q):
            second_sum[q] = (
                first_sum[q, c].astype(jnp.float32) + second[q].astype(jnp.float32)
            ).astype(jnp.bfloat16)

        for k in range(1, chips):
            third_copy((p + k) % chips).start()

    def finish_third():
        summed = second_sum[p].astype(jnp.float32)
        for k in range(1, chips):
            q = (p + k) % chips
            arrival(third, third_recv, q).wait()
            summed += third[q].astype(jnp.float32)
        total[...] = summed

    @pl.when(p < chips - 1)
    def _():
        line_copy(1, p).start()

    @pl.when(p > 0)
    def _():
        line_copy(0, p).start()

    sib_copy(p).start()
    hid_copy(sibling).start()

    def hid_start(k):
        for sign in (-1, 1):
            q = p + sign * k

            @pl.when(jnp.logical_and(q >= 0, q < chips))
            def _(q=q):
                hid_copy(2 * q + c).start()
                hid_copy(2 * q + 1 - c).start()

    for k in range(chips - 1, 1, -1):
        hid_start(k)

    @pl.loop(0, g_ref.shape[0] // 256)
    def _(i):
        at = pl.ds(pl.multiple_of(i * 256, 256), 256)
        g_ref[at, :] = lax.dot_general(
            dt_ref[:, at],
            low_ref[...],
            (((0,), (0,)), ((), ())),
            preferred_element_type=jnp.float32,
        ).astype(jnp.bfloat16)

    for k in range(1, groups):
        first_copy((e + k) % groups).start()

    acc[...] = jnp.zeros_like(acc)

    rows = min(256, cols)
    width = 512

    def multiply(s):
        @pl.loop(0, cols // rows)
        def _(i):
            at = pl.ds(pl.multiple_of(i * rows, rows), rows)
            left = hid[s, :, at]

            for j in range(acc.shape[1] // width):
                wide = pl.ds(j * width, width)
                acc[at, wide] += lax.dot_general(
                    left,
                    outs[s, :, wide],
                    (((0,), (0,)), ((), ())),
                    preferred_element_type=jnp.float32,
                )

    def forward(k):
        left, right = p - k, p + k

        @pl.when(left >= 0)
        def _():
            out_arrival(2 * left + c).wait()

            @pl.when(p < chips - 1)
            def _():
                line_copy(1, left).start()

            sib_copy(left).start()

        @pl.when(right < chips)
        def _():
            out_arrival(2 * right + c).wait()

            @pl.when(p > 0)
            def _():
                line_copy(0, right).start()

            sib_copy(right).start()

    def multiply_at(k):
        @pl.loop(0, 4)
        def _(j):
            q = p + (2 * (j // 2) - 1) * k
            cc = (c + j) % 2

            @pl.when(jnp.logical_and(q >= 0, q < chips))
            def _():
                s = 2 * q + cc

                @pl.when(cc != c)
                def _():
                    out_arrival(s).wait()

                hid_arrival(s).wait()
                multiply(s)

    own.wait()
    multiply(d)
    out_arrival(sibling).wait()
    hid_arrival(sibling).wait()
    multiply(sibling)

    @pl.loop(1, chips + 1)
    def _(k):
        @pl.when(k < chips)
        def _():
            forward(k)

            @pl.when(k == 1)
            def _():
                hid_start(1)

        @pl.when(k == 1)
        def _():
            finish_first()

        @pl.when(k == 2)
        def _():
            finish_second()

        @pl.when(k > 1)
        def _():
            multiply_at(k - 1)

    finish_third()

    @pl.loop(0, chips)
    def _(q):
        sib_copy(q).wait_send()

        @pl.when(jnp.logical_and(q <= p, p < chips - 1))
        def _():
            line_copy(1, q).wait_send()

        @pl.when(jnp.logical_and(q >= p, p > 0))
        def _():
            line_copy(0, q).wait_send()

    @pl.loop(1, n)
    def _(k):
        hid_copy((d + k) % n).wait_send()

    for k in range(1, groups):
        first_copy((e + k) % groups).wait_send()
    second_copy().wait_send()
    for k in range(1, chips):
        third_copy((p + k) % chips).wait_send()


def gradients(n, groups, counts, hidden, out_rows, dt_grads, low_rank):
    capacity, total = hidden.shape
    width = out_rows.shape[1]
    cols = total // n
    chips = n // 2
    inner, rank = dt_grads.shape[1], low_rank.shape[1]
    block = inner // (n * groups)
    return pl.pallas_call(
        functools.partial(expert_kernel, n, groups),
        out_shape=(
            jax.ShapeDtypeStruct((cols, width), jnp.float32),
            jax.ShapeDtypeStruct((block, rank), jnp.float32),
        ),
        in_specs=[
            pl.BlockSpec(memory_space=pltpu.SMEM),
            pl.BlockSpec(memory_space=pl.ANY),
            pl.BlockSpec(memory_space=pltpu.VMEM),
            pl.BlockSpec(memory_space=pltpu.VMEM),
            pl.BlockSpec(memory_space=pltpu.VMEM),
        ],
        out_specs=(
            pl.BlockSpec(memory_space=pltpu.VMEM),
            pl.BlockSpec(memory_space=pltpu.VMEM),
        ),
        scratch_shapes=[
            pltpu.VMEM((n, capacity, cols), jnp.bfloat16),
            pltpu.VMEM((n, capacity, width), jnp.bfloat16),
            pltpu.VMEM((groups, inner // groups, rank), jnp.bfloat16),
            pltpu.VMEM((chips, 2, block, rank), jnp.bfloat16),
            pltpu.VMEM((chips, block, rank), jnp.bfloat16),
            pltpu.VMEM((chips, block, rank), jnp.bfloat16),
            pltpu.VMEM((chips, block, rank), jnp.bfloat16),
            pltpu.VMEM((inner, rank), jnp.bfloat16),
            pltpu.SemaphoreType.DMA((n,)),
            pltpu.SemaphoreType.DMA((n,)),
            pltpu.SemaphoreType.DMA((2, chips)),
            pltpu.SemaphoreType.DMA((chips,)),
            pltpu.SemaphoreType.DMA((n,)),
            pltpu.SemaphoreType.DMA,
            pltpu.SemaphoreType.DMA((groups,)),
            pltpu.SemaphoreType.DMA((groups,)),
            pltpu.SemaphoreType.DMA,
            pltpu.SemaphoreType.DMA,
            pltpu.SemaphoreType.DMA((chips,)),
            pltpu.SemaphoreType.DMA((chips,)),
        ],
        compiler_params=pltpu.CompilerParams(
            collective_id=0, has_side_effects=True, vmem_limit_bytes=56 * 2**20
        ),
        cost_estimate=pl.CostEstimate(
            flops=2 * n * capacity * cols * width, bytes_accessed=600 * 2**20, transcendentals=0
        ),
    )(counts, hidden, out_rows, dt_grads, low_rank)


def body(
    n, groups, hidden_rows, out_grads, counts, expert_m, expert_v, low_rank, dt_grads, mamba_m, mamba_v
):
    expert_grad, mamba_grad = gradients(
        n, groups, counts, hidden_rows[0], out_grads[0], dt_grads, low_rank
    )
    moment_one, second, direction = adam_update(expert_m[0], expert_v[0], expert_grad)
    mamba_one, mamba_two, mamba_dir = adam_update(mamba_m, mamba_v, mamba_grad)
    return (
        moment_one.astype(jnp.bfloat16)[None],
        second.astype(jnp.bfloat16)[None],
        direction.astype(jnp.bfloat16)[None],
        mamba_one,
        mamba_two,
        mamba_dir,
    )


def solution(mesh):
    in_specs = (
        P("expert", "dp", None),
        P("expert", "dp", None),
        P("expert", "dp"),
        P("expert", "dp", None),
        P("expert", "dp", None),
        P(("expert", "dp"), None),
        P(("expert", "dp"), None),
        P(("expert", "dp"), None),
        P(("expert", "dp"), None),
    )
    out_specs = (
        P("expert", "dp", None),
        P("expert", "dp", None),
        P("expert", "dp", None),
        P(("expert", "dp"), None),
        P(("expert", "dp"), None),
        P(("expert", "dp"), None),
    )
    return jax.shard_map(
        functools.partial(body, mesh.shape["dp"], mesh.shape["expert"]),
        mesh=mesh,
        in_specs=in_specs,
        out_specs=out_specs,
        check_vma=False,
    )
```

```python
import functools

import jax
import jax.numpy as jnp
from jax import lax
from jax.experimental import pallas as pl
from jax.experimental.pallas import tpu as pltpu
from jax.sharding import PartitionSpec as P

STEP = 20
MESH = pl.DeviceIdType.MESH


def adam_update(moment_old, second_old, gradient):
    moment_one = 0.9 * moment_old.astype(jnp.float32) + 0.1 * gradient
    second = 0.999 * second_old.astype(jnp.float32) + 0.001 * gradient * gradient
    direction = moment_one / (1.0 - 0.9**STEP) / (jnp.sqrt(second / (1.0 - 0.999**STEP)) + 1e-08)
    return (moment_one, second, direction)


def expert_kernel(
    n,
    groups,
    count_ref,
    h_ref,
    o_ref,
    dt_ref,
    low_ref,
    acc,
    total,
    hid,
    outs,
    first,
    first_sum,
    second,
    second_sum,
    third,
    g_ref,
    hid_send,
    hid_recv,
    line_send,
    sib_send,
    out_recv,
    own_sem,
    first_send,
    first_recv,
    second_send,
    second_recv,
    third_send,
    third_recv,
):
    chips = n // 2
    d = lax.axis_index("dp")
    e = lax.axis_index("expert")
    p, c = d // 2, d % 2
    sibling = 2 * p + 1 - c
    capacity = o_ref.shape[0]
    cols = hid.shape[2]

    def columns(t):
        return pl.ds(pl.multiple_of(t * cols, cols), cols)

    own = pltpu.make_async_copy(h_ref.at[:, columns(d)], hid.at[d], own_sem)
    own.start()
    positions = lax.broadcasted_iota(jnp.int32, o_ref.shape, 0)
    value = o_ref[...]
    outs[d] = jnp.where(positions < count_ref[0, 0], value, jnp.zeros_like(value))

    barrier = pltpu.get_barrier_semaphore()
    for k in range(1, n):
        pl.semaphore_signal(barrier, inc=1, device_id={"dp": (d + k) % n}, device_id_type=MESH)
    for k in range(1, groups):
        pl.semaphore_signal(
            barrier, inc=1, device_id={"expert": (e + k) % groups}, device_id_type=MESH
        )
    pl.semaphore_wait(barrier, n + groups - 2)

    def line_copy(side, q, half):
        s = 2 * q + c
        part = pl.ds(half * (capacity // 2), capacity // 2)
        return pltpu.make_async_remote_copy(
            src_ref=outs.at[s, part],
            dst_ref=outs.at[s, part],
            send_sem=line_send.at[side, q, half],
            recv_sem=out_recv.at[half, s],
            device_id={"dp": d + (2 if side else -2)},
            device_id_type=MESH,
        )

    def sib_copy(q):
        s = 2 * q + c
        return pltpu.make_async_remote_copy(
            src_ref=outs.at[s],
            dst_ref=outs.at[s],
            send_sem=sib_send.at[q],
            recv_sem=out_recv.at[0, s],
            device_id={"dp": sibling},
            device_id_type=MESH,
        )

    def out_arrival(s):
        return pltpu.make_async_copy(outs.at[s], outs.at[s], out_recv.at[0, s])

    def half_arrival(s, half):
        part = outs.at[s, pl.ds(half * (capacity // 2), capacity // 2)]
        return pltpu.make_async_copy(part, part, out_recv.at[half, s])

    def hid_copy(t):
        return pltpu.make_async_remote_copy(
            src_ref=h_ref.at[:, columns(t)],
            dst_ref=hid.at[d],
            send_sem=hid_send.at[t],
            recv_sem=hid_recv.at[d],
            device_id={"dp": t},
            device_id_type=MESH,
        )

    def hid_arrival(s):
        return pltpu.make_async_copy(hid.at[s], hid.at[s], hid_recv.at[s])

    span = g_ref.shape[0] // groups
    block = total.shape[0]

    def first_copy(t):
        return pltpu.make_async_remote_copy(
            src_ref=g_ref.at[pl.ds(pl.multiple_of(t * span, span), span), :],
            dst_ref=first.at[e],
            send_sem=first_send.at[t],
            recv_sem=first_recv.at[e],
            device_id={"expert": t},
            device_id_type=MESH,
        )

    def second_copy():
        return pltpu.make_async_remote_copy(
            src_ref=first_sum.at[:, 1 - c],
            dst_ref=second,
            send_sem=second_send,
            recv_sem=second_recv,
            device_id={"dp": sibling},
            device_id_type=MESH,
        )

    def third_copy(q):
        return pltpu.make_async_remote_copy(
            src_ref=second_sum.at[q],
            dst_ref=third.at[p],
            send_sem=third_send.at[q],
            recv_sem=third_recv.at[p],
            device_id={"dp": 2 * q + c},
            device_id_type=MESH,
        )

    def arrival(buffer, sem, at):
        return pltpu.make_async_copy(buffer.at[at], buffer.at[at], sem.at[at])

    def finish_first():
        for k in range(1, groups):
            arrival(first, first_recv, (e + k) % groups).wait()

        @pl.loop(0, n)
        def _(t):
            summed = g_ref[
                pl.ds(pl.multiple_of(e * span + t * block, block), block), :
            ].astype(jnp.float32)
            for k in range(1, groups):
                summed += first[
                    (e + k) % groups, pl.ds(pl.multiple_of(t * block, block), block), :
                ].astype(jnp.float32)
            first_sum[t // 2, t % 2] = summed.astype(jnp.bfloat16)

        second_copy().start()

    def finish_second():
        pltpu.make_async_copy(second, second, second_recv).wait()

        @pl.loop(0, chips)
        def _(q):
            second_sum[q] = (
                first_sum[q, c].astype(jnp.float32) + second[q].astype(jnp.float32)
            ).astype(jnp.bfloat16)

        for k in range(1, chips):
            third_copy((p + k) % chips).start()

    def finish_third():
        summed = second_sum[p].astype(jnp.float32)
        for k in range(1, chips):
            q = (p + k) % chips
            arrival(third, third_recv, q).wait()
            summed += third[q].astype(jnp.float32)
        total[...] = summed

    @pl.when(p < chips - 1)
    def _():
        line_copy(1, p, 0).start()
        line_copy(1, p, 1).start()

    @pl.when(p > 0)
    def _():
        line_copy(0, p, 0).start()
        line_copy(0, p, 1).start()

    sib_copy(p).start()
    hid_copy(sibling).start()

    def hid_start(k):
        for sign in (-1, 1):
            q = p + sign * k

            @pl.when(jnp.logical_and(q >= 0, q < chips))
            def _(q=q):
                hid_copy(2 * q + c).start()
                hid_copy(2 * q + 1 - c).start()

    for k in range(chips - 1, 1, -1):
        hid_start(k)

    @pl.loop(0, g_ref.shape[0] // 256)
    def _(i):
        at = pl.ds(pl.multiple_of(i * 256, 256), 256)
        g_ref[at, :] = lax.dot_general(
            dt_ref[:, at],
            low_ref[...],
            (((0,), (0,)), ((), ())),
            preferred_element_type=jnp.float32,
        ).astype(jnp.bfloat16)

    for k in range(1, groups):
        first_copy((e + k) % groups).start()

    acc[...] = jnp.zeros_like(acc)

    rows = min(256, cols)
    width = 512

    def multiply(s):
        @pl.loop(0, cols // rows)
        def _(i):
            at = pl.ds(pl.multiple_of(i * rows, rows), rows)
            left = hid[s, :, at]

            for j in range(acc.shape[1] // width):
                wide = pl.ds(j * width, width)
                acc[at, wide] += lax.dot_general(
                    left,
                    outs[s, :, wide],
                    (((0,), (0,)), ((), ())),
                    preferred_element_type=jnp.float32,
                )

    def forward(k):
        left, right = p - k, p + k

        @pl.when(left >= 0)
        def _():
            for half in range(2):
                half_arrival(2 * left + c, half).wait()

                @pl.when(p < chips - 1)
                def _(half=half):
                    line_copy(1, left, half).start()

            sib_copy(left).start()

        @pl.when(right < chips)
        def _():
            for half in range(2):
                half_arrival(2 * right + c, half).wait()

                @pl.when(p > 0)
                def _(half=half):
                    line_copy(0, right, half).start()

            sib_copy(right).start()

    def multiply_at(k):
        @pl.loop(0, 4)
        def _(j):
            q = p + (2 * (j // 2) - 1) * k
            cc = (c + j) % 2

            @pl.when(jnp.logical_and(q >= 0, q < chips))
            def _():
                s = 2 * q + cc

                @pl.when(cc != c)
                def _():
                    out_arrival(s).wait()

                hid_arrival(s).wait()
                multiply(s)

    own.wait()
    multiply(d)
    out_arrival(sibling).wait()
    hid_arrival(sibling).wait()
    multiply(sibling)

    @pl.loop(1, chips + 1)
    def _(k):
        @pl.when(k < chips)
        def _():
            forward(k)

            @pl.when(k == 1)
            def _():
                hid_start(1)

        @pl.when(k == 1)
        def _():
            finish_first()

        @pl.when(k == 2)
        def _():
            finish_second()

        @pl.when(k > 1)
        def _():
            multiply_at(k - 1)

    finish_third()

    @pl.loop(0, chips)
    def _(q):
        sib_copy(q).wait_send()

        @pl.when(jnp.logical_and(q <= p, p < chips - 1))
        def _():
            line_copy(1, q, 0).wait_send()
            line_copy(1, q, 1).wait_send()

        @pl.when(jnp.logical_and(q >= p, p > 0))
        def _():
            line_copy(0, q, 0).wait_send()
            line_copy(0, q, 1).wait_send()

    @pl.loop(1, n)
    def _(k):
        hid_copy((d + k) % n).wait_send()

    for k in range(1, groups):
        first_copy((e + k) % groups).wait_send()
    second_copy().wait_send()
    for k in range(1, chips):
        third_copy((p + k) % chips).wait_send()


def gradients(n, groups, counts, hidden, out_rows, dt_grads, low_rank):
    capacity, total = hidden.shape
    width = out_rows.shape[1]
    cols = total // n
    chips = n // 2
    inner, rank = dt_grads.shape[1], low_rank.shape[1]
    block = inner // (n * groups)
    return pl.pallas_call(
        functools.partial(expert_kernel, n, groups),
        out_shape=(
            jax.ShapeDtypeStruct((cols, width), jnp.float32),
            jax.ShapeDtypeStruct((block, rank), jnp.float32),
        ),
        in_specs=[
            pl.BlockSpec(memory_space=pltpu.SMEM),
            pl.BlockSpec(memory_space=pl.ANY),
            pl.BlockSpec(memory_space=pltpu.VMEM),
            pl.BlockSpec(memory_space=pltpu.VMEM),
            pl.BlockSpec(memory_space=pltpu.VMEM),
        ],
        out_specs=(
            pl.BlockSpec(memory_space=pltpu.VMEM),
            pl.BlockSpec(memory_space=pltpu.VMEM),
        ),
        scratch_shapes=[
            pltpu.VMEM((n, capacity, cols), jnp.bfloat16),
            pltpu.VMEM((n, capacity, width), jnp.bfloat16),
            pltpu.VMEM((groups, inner // groups, rank), jnp.bfloat16),
            pltpu.VMEM((chips, 2, block, rank), jnp.bfloat16),
            pltpu.VMEM((chips, block, rank), jnp.bfloat16),
            pltpu.VMEM((chips, block, rank), jnp.bfloat16),
            pltpu.VMEM((chips, block, rank), jnp.bfloat16),
            pltpu.VMEM((inner, rank), jnp.bfloat16),
            pltpu.SemaphoreType.DMA((n,)),
            pltpu.SemaphoreType.DMA((n,)),
            pltpu.SemaphoreType.DMA((2, chips, 2)),
            pltpu.SemaphoreType.DMA((chips,)),
            pltpu.SemaphoreType.DMA((2, n)),
            pltpu.SemaphoreType.DMA,
            pltpu.SemaphoreType.DMA((groups,)),
            pltpu.SemaphoreType.DMA((groups,)),
            pltpu.SemaphoreType.DMA,
            pltpu.SemaphoreType.DMA,
            pltpu.SemaphoreType.DMA((chips,)),
            pltpu.SemaphoreType.DMA((chips,)),
        ],
        compiler_params=pltpu.CompilerParams(
            collective_id=0, has_side_effects=True, vmem_limit_bytes=56 * 2**20
        ),
        cost_estimate=pl.CostEstimate(
            flops=2 * n * capacity * cols * width, bytes_accessed=600 * 2**20, transcendentals=0
        ),
    )(counts, hidden, out_rows, dt_grads, low_rank)


def body(
    n, groups, hidden_rows, out_grads, counts, expert_m, expert_v, low_rank, dt_grads, mamba_m, mamba_v
):
    expert_grad, mamba_grad = gradients(
        n, groups, counts, hidden_rows[0], out_grads[0], dt_grads, low_rank
    )
    moment_one, second, direction = adam_update(expert_m[0], expert_v[0], expert_grad)
    mamba_one, mamba_two, mamba_dir = adam_update(mamba_m, mamba_v, mamba_grad)
    return (
        moment_one.astype(jnp.bfloat16)[None],
        second.astype(jnp.bfloat16)[None],
        direction.astype(jnp.bfloat16)[None],
        mamba_one,
        mamba_two,
        mamba_dir,
    )


def solution(mesh):
    in_specs = (
        P("expert", "dp", None),
        P("expert", "dp", None),
        P("expert", "dp"),
        P("expert", "dp", None),
        P("expert", "dp", None),
        P(("expert", "dp"), None),
        P(("expert", "dp"), None),
        P(("expert", "dp"), None),
        P(("expert", "dp"), None),
    )
    out_specs = (
        P("expert", "dp", None),
        P("expert", "dp", None),
        P("expert", "dp", None),
        P(("expert", "dp"), None),
        P(("expert", "dp"), None),
        P(("expert", "dp"), None),
    )
    return jax.shard_map(
        functools.partial(body, mesh.shape["dp"], mesh.shape["expert"]),
        mesh=mesh,
        in_specs=in_specs,
        out_specs=out_specs,
        check_vma=False,
    )
```
